256 devices in a mesh: wide: 32 (over y, z_lo, core), narrow: 8 (over z_hi, x).
Axes of the slice: x: 4, y: 4, z: 8 (z_hi: 2, z_lo: 4; z = z_hi * 4 + z_lo), core: 2. Of those that a mesh axis runs over, the one named last changes fastest.
Arguments:
- state: float32 [2, 33554432], P(None, ('wide', 'narrow')), may hold values from -6 to 6
- gate_re: float32 [6, 128, 128], replicated, may hold values from -0.375 to 0.375
- gate_im: float32 [6, 128, 128], replicated, may hold values from -0.375 to 0.375
- bit_orders: int32 [6, 8], replicated, may hold values from 0 to 7, each once within a row
- phase_pairs: int32 [6, 16, 2], replicated, may hold values from 0 to 11
- phase_angles: float32 [6, 16], replicated, may hold values from -3.140625 to 3.140625
Outputs:
- final_state: float32 [2, 33554432], P(None, ('wide', 'narrow'))
The draws below stay inside these ranges and needn't reach their ends.
Inputs may be any that keep to these rules, and one draw needn't show every extreme that they name: `bit_orders`: each row is a permutation of 0 to 7. `phase_pairs`: qubit positions among the lowest 12; the two of a pair may coincide.
All inputs are finite; a program needn't handle non-finite values.
Results may differ from the reference program's by a relative error of at most 0.00012.
Values sent between devices are 32-bit elements; how exact they have to be, the bound alone decides.
A program may use at most 64 MiB of HBM per device.

```python
from functools import partial
import jax
import jax.numpy as jnp
from jax import lax

LAYERS = 6
GATE = 128
PHASES = 16
PHASE_BITS = 12
AMPS = 33554432
ROWS_HIGH = 64
LOW_SPAN = 8
N_WIDE = 32
N_NARROW = 8


def touch_ends(entries, own_key, least, largest):
    dims = entries.shape
    place = [jax.random.randint(jax.random.fold_in(own_key, axis), (), 0, dims[axis]) for axis in range(len(dims))]
    entries = entries.at[tuple(place)].set(least)
    longest = dims.index(max(dims))
    place[longest] = (place[longest] + 1) % dims[longest]
    return entries.at[tuple(place)].set(largest)


def steps_of(own_key, extent, split, least, top_value):
    loudness = 1.0
    for axis_at, blocks in split:
        heights = jax.random.uniform(jax.random.fold_in(jax.random.fold_in(own_key, 6), axis_at), (blocks,), jnp.float32, least / len(split), top_value / len(split))
        loudness = loudness * jnp.repeat(jnp.exp(heights), extent[axis_at] // blocks).reshape((-1,) + (1,) * (len(extent) - 1 - axis_at))
    return loudness


def normal_values(key, dims, deviation, most, shards=(), kind=jnp.bfloat16):
    gain = steps_of(key, dims, shards, -0.22, 0.18) if shards else 1.0
    drawn = jax.random.normal(key, dims, jnp.float32) * deviation * gain
    return jnp.minimum(jnp.maximum(drawn, -most), most).astype(kind)


def setup_inputs(seed: int = 0) -> dict:
    keys = jax.random.split(jax.random.key(seed), 7)
    state = normal_values(keys[0], (2, AMPS), 1.0, 6.0, ((1, 256),), jnp.float32)
    gate_re = normal_values(keys[1], (LAYERS, GATE, GATE), (2 * GATE) ** -0.5, 0.375, (), jnp.float32)
    gate_im = normal_values(keys[2], (LAYERS, GATE, GATE), (2 * GATE) ** -0.5, 0.375, (), jnp.float32)
    bit_orders = jax.vmap(lambda own: jax.random.permutation(own, 8))(jax.random.split(keys[3], LAYERS)).reshape((LAYERS, 8)).astype(jnp.int32)
    phase_pairs = touch_ends(jax.random.randint(keys[4], (LAYERS, PHASES, 2), 0, PHASE_BITS), jax.random.fold_in(keys[4], 1), 0, PHASE_BITS - 1).astype(jnp.int32)
    phase_angles = jnp.clip(jax.random.uniform(keys[5], (LAYERS, PHASES), jnp.float32, -3.140625, 3.140625), -3.140625, 3.140625)
    return dict(state=state, gate_re=gate_re, gate_im=gate_im, bit_orders=bit_orders, phase_pairs=phase_pairs, phase_angles=phase_angles)


def source_index(bit_order):
    position = jnp.arange(256, dtype=jnp.int32)
    source = jnp.zeros((256,), jnp.int32)
    for which in range(8):
        source = source + jnp.left_shift(jnp.right_shift(position, which) & 1, bit_order[which])
    return source


def complex_rows(left_re, left_im, right_re, right_im):
    product = partial(jnp.dot, preferred_element_type=jnp.float32, precision=lax.Precision.HIGHEST)
    real = product(left_re, right_re.T) - product(left_im, right_im.T)
    imag = product(left_re, right_im.T) + product(left_im, right_re.T)
    return real, imag


def apply_gates(blocks, bit_order, matrix_re, matrix_im):
    moved = jnp.take(blocks, source_index(bit_order), axis=2)
    halves = moved.reshape(2, -1, 128)
    real, imag = complex_rows(halves[0], halves[1], matrix_re, matrix_im)
    return jnp.stack([real, imag]).reshape(blocks.shape)


def phase_factors(pair_row, angle_row):
    position = jnp.arange(2 ** PHASE_BITS, dtype=jnp.int32)
    first = jnp.right_shift(position[None, :], pair_row[:, 0:1]) & 1
    second = jnp.right_shift(position[None, :], pair_row[:, 1:2]) & 1
    phase = jnp.sum(angle_row[:, None] * (first * second).astype(jnp.float32), axis=0)
    return jnp.cos(phase), jnp.sin(phase)


def apply_phase(amps, pair_row, angle_row):
    cosine, sine = phase_factors(pair_row, angle_row)
    view = amps.reshape(2, -1, 2 ** PHASE_BITS)
    real = view[0] * cosine - view[1] * sine
    imag = view[0] * sine + view[1] * cosine
    return jnp.stack([real, imag]).reshape(amps.shape)


def reference(state, gate_re, gate_im, bit_orders, phase_pairs, phase_angles):
    amps = state
    for layer in range(LAYERS):
        view = amps.reshape(2, N_WIDE, N_NARROW, ROWS_HIGH, N_NARROW, N_WIDE, LOW_SPAN)
        amps = view.transpose(0, 5, 4, 3, 2, 1, 6).reshape(2, -1)
        blocks = amps.reshape(2, -1, 256)
        amps = apply_gates(blocks, bit_orders[layer], gate_re[layer], gate_im[layer]).reshape(2, -1)
        amps = apply_phase(amps, phase_pairs[layer], phase_angles[layer])
    return amps
```

```python
import jax
import jax.numpy as jnp
from jax import lax
from jax.experimental import pallas as pl
from jax.experimental.pallas import tpu as pltpu
from jax.sharding import PartitionSpec as P

LAYERS = 6
PHASES = 16
WIDE = 32
CHUNKS = 2
STEP_BITS = (2, 1, 3, 4, 0)


def dot_rows(left, right):
    return lax.dot_general(left, right, (((1,), (0,)), ((), ())), preferred_element_type=jnp.float32)


def split(values):
    high = values.astype(jnp.bfloat16)
    low = (values - high.astype(jnp.float32)).astype(jnp.bfloat16)
    return high, low


def transpose_granules(tiles):
    lane = lax.broadcasted_iota(jnp.int32, (8, 128), 1)
    skewed = [tiles[i] if i == 0 else pltpu.roll(tiles[i], 8 * i, 1) for i in range(16)]
    turned = [skewed[(-i) % 16] for i in range(16)]
    for bit in range(4):
        mask = (lane // (8 << bit)) % 2 == 1
        turned = [jnp.where(mask, turned[(i - (1 << bit)) % 16], turned[i]) for i in range(16)]
    return [turned[k] if k == 0 else pltpu.roll(turned[k], 128 - 8 * k, 1) for k in range(16)]


def partner(me, step):
    other = 0
    for source, target in enumerate(STEP_BITS):
        mine = (me // (1 << target)) % 2
        flip = (step // (1 << source)) % 2
        other = other + ((mine + flip) % 2) * (1 << target)
    return other


def kernel(
    bit_orders,
    phase_pairs,
    phase_angles,
    gate_re,
    gate_im,
    given,
    result,
    landed,
    leaving,
    held,
    product,
    weight_high,
    weight_low,
    cosines,
    sines,
    in_send,
    in_recv,
    out_send,
    out_recv,
    own_sem,
):
    me = lax.axis_index("wide")
    narrow = lax.axis_index("narrow")
    barrier = pltpu.get_barrier_semaphore()

    def greet(step, carry):
        pl.semaphore_signal(
            barrier, inc=1, device_id={"wide": partner(me, step)}, device_id_type=pl.DeviceIdType.MESH
        )
        return carry

    lax.fori_loop(1, WIDE, greet, 0)
    pl.semaphore_wait(barrier, WIDE - 1)

    def send_in(chunk):
        def one(step, carry):
            other = partner(me, step)
            pltpu.make_async_remote_copy(
                src_ref=given.at[other, chunk],
                dst_ref=landed.at[chunk, me],
                send_sem=in_send,
                recv_sem=in_recv.at[chunk],
                device_id={"wide": other},
                device_id_type=pl.DeviceIdType.MESH,
            ).start()
            return carry

        lax.fori_loop(1, WIDE, one, 0)

    for chunk in range(CHUNKS):
        send_in(chunk)
    for chunk in range(CHUNKS):
        pltpu.make_async_copy(given.at[me, chunk], landed.at[chunk, me], own_sem.at[chunk]).start()

    def build(layer, carry):
        gr_high, gr_low = split(gate_re[layer])
        gi_high, gi_low = split(gate_im[layer])
        lanes = lax.broadcasted_iota(jnp.int32, (128, 128), 1)
        rows = lax.broadcasted_iota(jnp.int32, (128, 128), 0)
        base = jnp.zeros((128, 128), jnp.int32)
        for which in range(7):
            base = base + jnp.left_shift(jnp.right_shift(lanes, which) & 1, bit_orders[layer, which])
        top = jnp.left_shift(jnp.int32(1), bit_orders[layer, 7])
        for h in range(2):
            for e in range(2):
                source = base + e * top
                picks = jnp.where(rows + h * 128 == source, 1.0, 0.0).astype(jnp.bfloat16)
                for store, re, im in ((weight_high, gr_high, gi_high), (weight_low, gr_low, gi_low)):
                    real = lax.dot_general(
                        picks, re, (((1,), (1,)), ((), ())), preferred_element_type=jnp.float32
                    ).astype(jnp.bfloat16)
                    imag = lax.dot_general(
                        picks, im, (((1,), (1,)), ((), ())), preferred_element_type=jnp.float32
                    ).astype(jnp.bfloat16)
                    store[layer, pl.ds(h * 256, 128), pl.ds(e * 256, 128)] = real
                    store[layer, pl.ds(h * 256, 128), pl.ds(e * 256 + 128, 128)] = imag
                    store[layer, pl.ds(h * 256 + 128, 128), pl.ds(e * 256, 128)] = -imag
                    store[layer, pl.ds(h * 256 + 128, 128), pl.ds(e * 256 + 128, 128)] = real
        return carry

    lax.fori_loop(0, LAYERS, build, 0)

    lane = lax.broadcasted_iota(jnp.int32, (8, 128), 1)
    sublane = lax.broadcasted_iota(jnp.int32, (8, 128), 0)

    def phases(layer, carry):
        odd = layer % 2
        middle = odd * sublane + (1 - odd) * narrow
        low = middle * 256 + lane
        for chunk in range(CHUNKS):
            for h in range(2):
                position = low + (chunk * 2048 + h * 128)
                phi = jnp.zeros((8, 128), jnp.float32)
                for gate in range(PHASES):
                    first = jnp.right_shift(position, phase_pairs[layer, gate, 0])
                    second = jnp.right_shift(position, phase_pairs[layer, gate, 1])
                    phi = phi + phase_angles[layer, gate] * (first & second & 1).astype(jnp.float32)
                cosines[layer, chunk, h] = jnp.cos(phi)
                sines[layer, chunk, h] = jnp.sin(phi)
        return carry

    lax.fori_loop(0, LAYERS, phases, 0)

    def one_chunk(chunk, carry):
        arrivals = landed.at[chunk, pl.ds(0, WIDE - 1)]
        pltpu.make_async_copy(arrivals, arrivals, in_recv.at[chunk]).wait()
        pltpu.make_async_copy(given.at[me, chunk], landed.at[chunk, me], own_sem.at[chunk]).wait()

        for a_high in range(2):
            for a2_high in range(2):
                for part in range(2):
                    tiles = [landed[chunk, a_high * 16 + i, a2_high * 2 + part] for i in range(16)]
                    tiles = transpose_granules(tiles)
                    for i in range(16):
                        held[a_high * 2 + part, pl.ds((a2_high * 16 + i) * 8, 8), :] = tiles[i]

        for layer in range(LAYERS):
            x = jnp.concatenate([held[k] for k in range(4)], axis=1)
            high, low = split(x)
            w_high = weight_high[layer]
            w_low = weight_low[layer]
            product[...] = dot_rows(high, w_high) + (dot_rows(low, w_high) + dot_rows(high, w_low))
            for h in range(2):
                cosine = cosines[layer, chunk, h]
                sine = sines[layer, chunk, h]
                for s in range(2):
                    reals = []
                    imags = []
                    for i in range(16):
                        rows = pl.ds((s * 16 + i) * 8, 8)
                        re = product[rows, pl.ds(h * 256, 128)]
                        im = product[rows, pl.ds(h * 256 + 128, 128)]
                        reals.append(re * cosine - im * sine)
                        imags.append(re * sine + im * cosine)
                    if layer < LAYERS - 1:
                        reals = transpose_granules(reals)
                        imags = transpose_granules(imags)
                        for i in range(16):
                            rows = pl.ds((h * 16 + i) * 8, 8)
                            held[s * 2, rows, :] = reals[i]
                            held[s * 2 + 1, rows, :] = imags[i]
                    else:
                        for i in range(16):
                            leaving[chunk, s * 16 + i, h * 2] = reals[i]
                            leaving[chunk, s * 16 + i, h * 2 + 1] = imags[i]

        def one(step, inner):
            other = partner(me, step)
            pltpu.make_async_remote_copy(
                src_ref=leaving.at[chunk, other],
                dst_ref=result.at[me, chunk],
                send_sem=out_send,
                recv_sem=out_recv,
                device_id={"wide": other},
                device_id_type=pl.DeviceIdType.MESH,
            ).start()
            return inner

        lax.fori_loop(1, WIDE, one, 0)
        pltpu.make_async_copy(leaving.at[chunk, me], result.at[me, chunk], own_sem.at[CHUNKS + chunk]).start()
        return carry

    lax.fori_loop(0, CHUNKS, one_chunk, 0)

    sent = given.at[pl.ds(0, WIDE - 1)]
    pltpu.make_async_copy(sent, sent, in_send).wait()
    for chunk in range(CHUNKS):
        pltpu.make_async_copy(leaving.at[chunk, me], result.at[me, chunk], own_sem.at[CHUNKS + chunk]).wait()
    arrived = result.at[pl.ds(0, WIDE - 1)]
    pltpu.make_async_copy(arrived, arrived, out_recv).wait()
    pltpu.make_async_copy(arrived, arrived, out_send).wait()


def run(given, bit_orders, phase_pairs, phase_angles, gate_re, gate_im):
    smem = pl.BlockSpec(memory_space=pltpu.SMEM)
    vmem = pl.BlockSpec(memory_space=pltpu.VMEM)
    return pl.pallas_call(
        kernel,
        out_shape=jax.ShapeDtypeStruct((WIDE, CHUNKS, 4, 8, 128), jnp.float32),
        in_specs=[smem, smem, smem, vmem, vmem, vmem],
        out_specs=vmem,
        scratch_shapes=[
            pltpu.VMEM((CHUNKS, WIDE, 4, 8, 128), jnp.float32),
            pltpu.VMEM((CHUNKS, WIDE, 4, 8, 128), jnp.float32),
            pltpu.VMEM((4, 256, 128), jnp.float32),
            pltpu.VMEM((256, 512), jnp.float32),
            pltpu.VMEM((LAYERS, 512, 512), jnp.bfloat16),
            pltpu.VMEM((LAYERS, 512, 512), jnp.bfloat16),
            pltpu.VMEM((LAYERS, CHUNKS, 2, 8, 128), jnp.float32),
            pltpu.VMEM((LAYERS, CHUNKS, 2, 8, 128), jnp.float32),
            pltpu.SemaphoreType.DMA,
            pltpu.SemaphoreType.DMA((CHUNKS,)),
            pltpu.SemaphoreType.DMA,
            pltpu.SemaphoreType.DMA,
            pltpu.SemaphoreType.DMA((2 * CHUNKS,)),
        ],
        compiler_params=pltpu.CompilerParams(
            collective_id=0, has_side_effects=True, vmem_limit_bytes=32 * 1024 * 1024
        ),
        cost_estimate=pl.CostEstimate(flops=4_831_838_208, bytes_accessed=4_194_304, transcendentals=49_152),
    )(bit_orders, phase_pairs, phase_angles, gate_re, gate_im, given)


def local(state, gate_re, gate_im, bit_orders, phase_pairs, phase_angles):
    view = state.reshape(2, WIDE, CHUNKS, 8, 2, 128)
    given = view.transpose(1, 2, 4, 0, 3, 5).reshape(WIDE, CHUNKS, 4, 8, 128)
    result = run(given, bit_orders, phase_pairs, phase_angles, gate_re, gate_im)
    back = result.reshape(WIDE, CHUNKS, 2, 2, 8, 128).transpose(3, 0, 1, 4, 2, 5)
    return back.reshape(state.shape)


def solution(mesh):
    return jax.shard_map(
        local,
        mesh=mesh,
        in_specs=(P(None, ("wide", "narrow")), P(), P(), P(), P(), P()),
        out_specs=P(None, ("wide", "narrow")),
        check_vma=False,
    )
```

```python
import jax
import jax.numpy as jnp
from jax import lax
from jax.experimental import pallas as pl
from jax.experimental.pallas import tpu as pltpu
from jax.sharding import PartitionSpec as P

LAYERS = 6
PHASES = 16
WIDE = 32
CHUNKS = 2
NEAR = [k for k in range(1, 32) if not k & 4]
FAR = [k for k in range(1, 32) if k & 4]
ORDERS = (list(range(1, 32)),) * 4


def dot_rows(left, right):
    return lax.dot_general(left, right, (((1,), (0,)), ((), ())), preferred_element_type=jnp.float32)


def split(values):
    high = values.astype(jnp.bfloat16)
    low = (values - high.astype(jnp.float32)).astype(jnp.bfloat16)
    return high, low


def transpose_granules(tiles):
    lane = lax.broadcasted_iota(jnp.int32, (8, 128), 1)
    skewed = [tiles[i] if i == 0 else pltpu.roll(tiles[i], 8 * i, 1) for i in range(16)]
    turned = [skewed[(-i) % 16] for i in range(16)]
    for bit in range(4):
        mask = (lane // (8 << bit)) % 2 == 1
        turned = [jnp.where(mask, turned[(i - (1 << bit)) % 16], turned[i]) for i in range(16)]
    return [turned[k] if k == 0 else pltpu.roll(turned[k], 128 - 8 * k, 1) for k in range(16)]


def partners(me):
    turns = [(1 - 2 * ((me // (1 << bit)) % 2)) * (1 << bit) for bit in range(5)]
    return [me + sum(turns[bit] for bit in range(5) if (distance >> bit) & 1) for distance in range(WIDE)]


def kernel(
    given,
    gate_re_given,
    gate_im_given,
    bit_orders_given,
    phase_pairs_given,
    phase_angles_given,
    result,
    gate_re,
    gate_im,
    bit_orders,
    phase_pairs,
    phase_angles,
    landed,
    leaving,
    held,
    product,
    weight_high,
    weight_low,
    cosines,
    sines,
    in_send,
    in_recv,
    out_send,
    out_recv,
    own_sem,
    fetch_sem,
):
    me = lax.axis_index("wide")
    narrow = lax.axis_index("narrow")
    barrier = pltpu.get_barrier_semaphore()

    others = partners(me)
    for distance in range(1, WIDE):
        pl.semaphore_signal(
            barrier, inc=1, device_id={"wide": others[distance]}, device_id_type=pl.DeviceIdType.MESH
        )
    parameters = [
        pltpu.make_async_copy(source, target, fetch_sem.at[i])
        for i, (source, target) in enumerate(
            [
                (gate_re_given, gate_re),
                (gate_im_given, gate_im),
                (bit_orders_given, bit_orders),
                (phase_pairs_given, phase_pairs),
                (phase_angles_given, phase_angles),
            ]
        )
    ]
    for copy in parameters:
        copy.start()
    pl.semaphore_wait(barrier, WIDE - 1)

    for chunk in range(CHUNKS):
        for distance in ORDERS[chunk]:
            pltpu.make_async_remote_copy(
                src_ref=given.at[others[distance], chunk],
                dst_ref=landed.at[chunk, me],
                send_sem=in_send,
                recv_sem=in_recv.at[chunk],
                device_id={"wide": others[distance]},
                device_id_type=pl.DeviceIdType.MESH,
            ).start()
    for chunk in range(CHUNKS):
        pltpu.make_async_copy(given.at[me, chunk], landed.at[chunk, me], own_sem.at[chunk]).start()

    for copy in parameters:
        copy.wait()

    def build(layer, carry):
        gr_high, gr_low = split(gate_re[layer])
        gi_high, gi_low = split(gate_im[layer])
        lanes = lax.broadcasted_iota(jnp.int32, (128, 128), 1)
        rows = lax.broadcasted_iota(jnp.int32, (128, 128), 0)
        base = jnp.zeros((128, 128), jnp.int32)
        for which in range(7):
            base = base + jnp.left_shift(jnp.right_shift(lanes, which) & 1, bit_orders[layer, which])
        top = jnp.left_shift(jnp.int32(1), bit_orders[layer, 7])
        for h in range(2):
            for e in range(2):
                source = base + e * top
                picks = jnp.where(rows + h * 128 == source, 1.0, 0.0).astype(jnp.bfloat16)
                for store, re, im in ((weight_high, gr_high, gi_high), (weight_low, gr_low, gi_low)):
                    real = lax.dot_general(
                        picks, re, (((1,), (1,)), ((), ())), preferred_element_type=jnp.float32
                    ).astype(jnp.bfloat16)
                    imag = lax.dot_general(
                        picks, im, (((1,), (1,)), ((), ())), preferred_element_type=jnp.float32
                    ).astype(jnp.bfloat16)
                    store[layer, pl.ds(h * 256, 128), pl.ds(e * 256, 128)] = real
                    store[layer, pl.ds(h * 256, 128), pl.ds(e * 256 + 128, 128)] = imag
                    store[layer, pl.ds(h * 256 + 128, 128), pl.ds(e * 256, 128)] = -imag
                    store[layer, pl.ds(h * 256 + 128, 128), pl.ds(e * 256 + 128, 128)] = real
        return carry

    lax.fori_loop(0, LAYERS, build, 0)

    lane = lax.broadcasted_iota(jnp.int32, (8, 128), 1)
    sublane = lax.broadcasted_iota(jnp.int32, (8, 128), 0)

    def phases(layer, carry):
        odd = layer % 2
        middle = odd * sublane + (1 - odd) * narrow
        low = middle * 256 + lane
        for chunk in range(CHUNKS):
            for h in range(2):
                position = low + (chunk * 2048 + h * 128)
                phi = jnp.zeros((8, 128), jnp.float32)
                for gate in range(PHASES):
                    first = jnp.right_shift(position, phase_pairs[layer, 0, gate])
                    second = jnp.right_shift(position, phase_pairs[layer, 1, gate])
                    phi = phi + phase_angles[layer, gate] * (first & second & 1).astype(jnp.float32)
                cosines[layer, chunk, h] = jnp.cos(phi)
                sines[layer, chunk, h] = jnp.sin(phi)
        return carry

    lax.fori_loop(0, LAYERS, phases, 0)

    def one_chunk(chunk, carry):
        arrivals = landed.at[chunk, pl.ds(0, WIDE - 1)]
        pltpu.make_async_copy(arrivals, arrivals, in_recv.at[chunk]).wait()
        pltpu.make_async_copy(given.at[me, chunk], landed.at[chunk, me], own_sem.at[chunk]).wait()

        for a_high in range(2):
            for a2_high in range(2):
                for part in range(2):
                    rows = pl.ds(a2_high * 2 + part, 8, stride=4)
                    tiles = [landed[chunk, a_high * 16 + i, rows, :] for i in range(16)]
                    tiles = transpose_granules(tiles)
                    for i in range(16):
                        held[a_high * 2 + part, pl.ds((a2_high * 16 + i) * 8, 8), :] = tiles[i]

        for layer in range(LAYERS):
            x = jnp.concatenate([held[k] for k in range(4)], axis=1)
            high, low = split(x)
            w_high = weight_high[layer]
            w_low = weight_low[layer]
            product[...] = dot_rows(high, w_high) + (dot_rows(low, w_high) + dot_rows(high, w_low))
            for h in range(2):
                cosine = cosines[layer, chunk, h]
                sine = sines[layer, chunk, h]
                for s in range(2):
                    reals = []
                    imags = []
                    for i in range(16):
                        rows = pl.ds((s * 16 + i) * 8, 8)
                        re = product[rows, pl.ds(h * 256, 128)]
                        im = product[rows, pl.ds(h * 256 + 128, 128)]
                        reals.append(re * cosine - im * sine)
                        imags.append(re * sine + im * cosine)
                    if layer < LAYERS - 1:
                        reals = transpose_granules(reals)
                        imags = transpose_granules(imags)
                        for i in range(16):
                            rows = pl.ds((h * 16 + i) * 8, 8)
                            held[s * 2, rows, :] = reals[i]
                            held[s * 2 + 1, rows, :] = imags[i]
                    else:
                        for i in range(16):
                            leaving[chunk, s * 16 + i, pl.ds(h * 2, 8, stride=4), :] = reals[i]
                            leaving[chunk, s * 16 + i, pl.ds(h * 2 + 1, 8, stride=4), :] = imags[i]

        for distance in ORDERS[2]:
            pltpu.make_async_remote_copy(
                src_ref=leaving.at[chunk, others[distance]],
                dst_ref=result.at[me, chunk],
                send_sem=out_send,
                recv_sem=out_recv,
                device_id={"wide": others[distance]},
                device_id_type=pl.DeviceIdType.MESH,
            ).start()
        pltpu.make_async_copy(leaving.at[chunk, me], result.at[me, chunk], own_sem.at[CHUNKS + chunk]).start()
        return carry

    lax.fori_loop(0, CHUNKS, one_chunk, 0)

    sent = given.at[pl.ds(0, WIDE - 1)]
    pltpu.make_async_copy(sent, sent, in_send).wait()
    for chunk in range(CHUNKS):
        pltpu.make_async_copy(leaving.at[chunk, me], result.at[me, chunk], own_sem.at[CHUNKS + chunk]).wait()
    arrived = result.at[pl.ds(0, WIDE - 1)]
    pltpu.make_async_copy(arrived, arrived, out_recv).wait()
    pltpu.make_async_copy(arrived, arrived, out_send).wait()


def run(given, gate_re, gate_im, bit_orders, phase_pairs, phase_angles):
    operands = (given, gate_re, gate_im, bit_orders, phase_pairs, phase_angles)
    return pl.pallas_call(
        kernel,
        out_shape=pltpu.VMEM(given.shape, jnp.float32),
        in_specs=[pl.BlockSpec(memory_space=pltpu.HBM)] * len(operands),
        out_specs=pl.BlockSpec(memory_space=pltpu.VMEM),
        scratch_shapes=[
            pltpu.VMEM(gate_re.shape, jnp.float32),
            pltpu.VMEM(gate_im.shape, jnp.float32),
            pltpu.SMEM(bit_orders.shape, jnp.int32),
            pltpu.SMEM(phase_pairs.shape, jnp.int32),
            pltpu.SMEM(phase_angles.shape, jnp.float32),
            pltpu.VMEM((CHUNKS, WIDE, 32, 128), jnp.float32),
            pltpu.VMEM((CHUNKS, WIDE, 32, 128), jnp.float32),
            pltpu.VMEM((4, 256, 128), jnp.float32),
            pltpu.VMEM((256, 512), jnp.float32),
            pltpu.VMEM((LAYERS, 512, 512), jnp.bfloat16),
            pltpu.VMEM((LAYERS, 512, 512), jnp.bfloat16),
            pltpu.VMEM((LAYERS, CHUNKS, 2, 8, 128), jnp.float32),
            pltpu.VMEM((LAYERS, CHUNKS, 2, 8, 128), jnp.float32),
            pltpu.SemaphoreType.DMA,
            pltpu.SemaphoreType.DMA((CHUNKS,)),
            pltpu.SemaphoreType.DMA,
            pltpu.SemaphoreType.DMA,
            pltpu.SemaphoreType.DMA((2 * CHUNKS,)),
            pltpu.SemaphoreType.DMA((5,)),
        ],
        compiler_params=pltpu.CompilerParams(
            collective_id=0, has_side_effects=True, vmem_limit_bytes=48 * 1024 * 1024
        ),
        cost_estimate=pl.CostEstimate(flops=4_831_838_208, bytes_accessed=4_194_304, transcendentals=49_152),
    )(*[pltpu.with_memory_space_constraint(x, pltpu.HBM) for x in operands])


def local(state, gate_re, gate_im, bit_orders, phase_pairs, phase_angles):
    given = state.reshape(2, 1024, 128).transpose(1, 0, 2).reshape(WIDE, CHUNKS, 32, 128)
    result = run(given, gate_re, gate_im, bit_orders, phase_pairs.transpose(0, 2, 1), phase_angles)
    return result.reshape(1024, 2, 128).transpose(1, 0, 2).reshape(state.shape)


def solution(mesh):
    return jax.shard_map(
        local,
        mesh=mesh,
        in_specs=(P(None, ("wide", "narrow")), P(), P(), P(), P(), P()),
        out_specs=P(None, ("wide", "narrow")),
        check_vma=False,
    )
```

```python
import jax
import jax.numpy as jnp
from jax import lax
from jax.experimental import pallas as pl
from jax.experimental.pallas import tpu as pltpu
from jax.sharding import PartitionSpec as P

LAYERS = 6
PHASES = 16
WIDE = 32
CHUNKS = 2


def dot_rows(left, right):
    return lax.dot_general(left, right, (((1,), (0,)), ((), ())), preferred_element_type=jnp.float32)


def split(values):
    high = values.astype(jnp.bfloat16)
    low = (values - high.astype(jnp.float32)).astype(jnp.bfloat16)
    return high, low


def transpose_granules(tiles):
    lane = lax.broadcasted_iota(jnp.int32, (8, 128), 1)
    skewed = [tiles[i] if i == 0 else pltpu.roll(tiles[i], 8 * i, 1) for i in range(16)]
    turned = [skewed[(-i) % 16] for i in range(16)]
    for bit in range(4):
        mask = (lane // (8 << bit)) % 2 == 1
        turned = [jnp.where(mask, turned[(i - (1 << bit)) % 16], turned[i]) for i in range(16)]
    return [turned[k] if k == 0 else pltpu.roll(turned[k], 128 - 8 * k, 1) for k in range(16)]


def partners(me):
    turns = [(1 - 2 * ((me // (1 << bit)) % 2)) * (1 << bit) for bit in range(5)]
    return [me + sum(turns[bit] for bit in range(5) if (distance >> bit) & 1) for distance in range(WIDE)]


def kernel(
    given_there,
    gate_re_given,
    gate_im_given,
    bit_orders_given,
    phase_pairs_given,
    phase_angles_given,
    result,
    gate_re,
    gate_im,
    bit_orders,
    phase_pairs,
    phase_angles,
    landed,
    leaving,
    held,
    product,
    weight_high,
    weight_low,
    cosines,
    sines,
    in_send,
    in_recv,
    out_send,
    out_recv,
    own_sem,
    fetch_sem,
    given,
):
    me = lax.axis_index("wide")
    narrow = lax.axis_index("narrow")
    barrier = pltpu.get_barrier_semaphore()

    others = partners(me)
    swing = (me // 2) % 2
    turned = partners(me + swing * 4 * (1 - 2 * ((me // 4) % 2)))
    sequence = [turned[i] for i in range(WIDE - 1, 0, -1) if i != 4] + [others[4]]
    for distance in range(WIDE - 1, 0, -1):
        pl.semaphore_signal(
            barrier, inc=1, device_id={"wide": others[distance]}, device_id_type=pl.DeviceIdType.MESH
        )
    parameters = [
        pltpu.make_async_copy(source, target, fetch_sem.at[i])
        for i, (source, target) in enumerate(
            [
                (gate_re_given, gate_re),
                (gate_im_given, gate_im),
                (bit_orders_given, bit_orders),
                (phase_pairs_given, phase_pairs),
                (phase_angles_given, phase_angles),
                (given_there, given),
            ]
        )
    ]
    for copy in parameters[::-1]:
        copy.start()
    parameters[5].wait()
    pl.semaphore_wait(barrier, WIDE - 1)

    for chunk in range(CHUNKS):
        for other in sequence:
            pltpu.make_async_remote_copy(
                src_ref=given.at[other, chunk],
                dst_ref=landed.at[chunk, me],
                send_sem=in_send,
                recv_sem=in_recv.at[chunk],
                device_id={"wide": other},
                device_id_type=pl.DeviceIdType.MESH,
            ).start()
    for chunk in range(CHUNKS):
        pltpu.make_async_copy(given.at[me, chunk], landed.at[chunk, me], own_sem.at[chunk]).start()

    for copy in parameters[:5]:
        copy.wait()

    def build(layer, carry):
        gr_high, gr_low = split(gate_re[layer])
        gi_high, gi_low = split(gate_im[layer])
        lanes = lax.broadcasted_iota(jnp.int32, (128, 128), 1)
        rows = lax.broadcasted_iota(jnp.int32, (128, 128), 0)
        base = jnp.zeros((128, 128), jnp.int32)
        for which in range(7):
            base = base + jnp.left_shift(jnp.right_shift(lanes, which) & 1, bit_orders[layer, which])
        top = jnp.left_shift(jnp.int32(1), bit_orders[layer, 7])
        for h in range(2):
            for e in range(2):
                source = base + e * top
                picks = jnp.where(rows + h * 128 == source, 1.0, 0.0).astype(jnp.bfloat16)
                for store, re, im in ((weight_high, gr_high, gi_high), (weight_low, gr_low, gi_low)):
                    real = lax.dot_general(
                        picks, re, (((1,), (1,)), ((), ())), preferred_element_type=jnp.float32
                    ).astype(jnp.bfloat16)
                    imag = lax.dot_general(
                        picks, im, (((1,), (1,)), ((), ())), preferred_element_type=jnp.float32
                    ).astype(jnp.bfloat16)
                    store[layer, pl.ds(h * 256, 128), pl.ds(e * 256, 128)] = real
                    store[layer, pl.ds(h * 256, 128), pl.ds(e * 256 + 128, 128)] = imag
                    store[layer, pl.ds(h * 256 + 128, 128), pl.ds(e * 256, 128)] = -imag
                    store[layer, pl.ds(h * 256 + 128, 128), pl.ds(e * 256 + 128, 128)] = real
        return carry

    lax.fori_loop(0, LAYERS, build, 0)

    lane = lax.broadcasted_iota(jnp.int32, (8, 128), 1)
    sublane = lax.broadcasted_iota(jnp.int32, (8, 128), 0)

    def phases(layer, carry):
        odd = layer % 2
        middle = odd * sublane + (1 - odd) * narrow
        low = middle * 256 + lane
        for chunk in range(CHUNKS):
            for h in range(2):
                position = low + (chunk * 2048 + h * 128)
                phi = jnp.zeros((8, 128), jnp.float32)
                for gate in range(PHASES):
                    first = jnp.right_shift(position, phase_pairs[layer, 0, gate])
                    second = jnp.right_shift(position, phase_pairs[layer, 1, gate])
                    phi = phi + phase_angles[layer, gate] * (first & second & 1).astype(jnp.float32)
                cosines[layer, chunk, h] = jnp.cos(phi)
                sines[layer, chunk, h] = jnp.sin(phi)
        return carry

    lax.fori_loop(0, LAYERS, phases, 0)

    def one_chunk(chunk, carry):
        arrivals = landed.at[chunk, pl.ds(0, WIDE - 1)]
        pltpu.make_async_copy(arrivals, arrivals, in_recv.at[chunk]).wait()
        pltpu.make_async_copy(given.at[me, chunk], landed.at[chunk, me], own_sem.at[chunk]).wait()

        for a_high in range(2):
            for a2_high in range(2):
                for part in range(2):
                    rows = pl.ds(a2_high * 2 + part, 8, stride=4)
                    tiles = [landed[chunk, a_high * 16 + i, rows, :] for i in range(16)]
                    tiles = transpose_granules(tiles)
                    for i in range(16):
                        held[a_high * 2 + part, pl.ds((a2_high * 16 + i) * 8, 8), :] = tiles[i]

        for layer in range(LAYERS):
            x = jnp.concatenate([held[k] for k in range(4)], axis=1)
            high, low = split(x)
            w_high = weight_high[layer]
            w_low = weight_low[layer]
            product[...] = dot_rows(high, w_high) + (dot_rows(low, w_high) + dot_rows(high, w_low))
            for h in range(2):
                cosine = cosines[layer, chunk, h]
                sine = sines[layer, chunk, h]
                for s in range(2):
                    reals = []
                    imags = []
                    for i in range(16):
                        rows = pl.ds((s * 16 + i) * 8, 8)
                        re = product[rows, pl.ds(h * 256, 128)]
                        im = product[rows, pl.ds(h * 256 + 128, 128)]
                        reals.append(re * cosine - im * sine)
                        imags.append(re * sine + im * cosine)
                    if layer < LAYERS - 1:
                        reals = transpose_granules(reals)
                        imags = transpose_granules(imags)
                        for i in range(16):
                            rows = pl.ds((h * 16 + i) * 8, 8)
                            held[s * 2, rows, :] = reals[i]
                            held[s * 2 + 1, rows, :] = imags[i]
                    else:
                        for i in range(16):
                            leaving[chunk, s * 16 + i, pl.ds(h * 2, 8, stride=4), :] = reals[i]
                            leaving[chunk, s * 16 + i, pl.ds(h * 2 + 1, 8, stride=4), :] = imags[i]

        for other in sequence:
            pltpu.make_async_remote_copy(
                src_ref=leaving.at[chunk, other],
                dst_ref=result.at[me, chunk],
                send_sem=out_send,
                recv_sem=out_recv,
                device_id={"wide": other},
                device_id_type=pl.DeviceIdType.MESH,
            ).start()
        pltpu.make_async_copy(leaving.at[chunk, me], result.at[me, chunk], own_sem.at[CHUNKS + chunk]).start()
        return carry

    lax.fori_loop(0, CHUNKS, one_chunk, 0)

    sent = given.at[pl.ds(0, WIDE - 1)]
    pltpu.make_async_copy(sent, sent, in_send).wait()
    for chunk in range(CHUNKS):
        pltpu.make_async_copy(leaving.at[chunk, me], result.at[me, chunk], own_sem.at[CHUNKS + chunk]).wait()
    arrived = result.at[pl.ds(0, WIDE - 1)]
    pltpu.make_async_copy(arrived, arrived, out_recv).wait()
    pltpu.make_async_copy(arrived, arrived, out_send).wait()


def run(given, gate_re, gate_im, bit_orders, phase_pairs, phase_angles):
    operands = (given, gate_re, gate_im, bit_orders, phase_pairs, phase_angles)
    return pl.pallas_call(
        kernel,
        out_shape=pltpu.VMEM(given.shape, jnp.float32),
        in_specs=[pl.BlockSpec(memory_space=pltpu.HBM)] * len(operands),
        out_specs=pl.BlockSpec(memory_space=pltpu.VMEM),
        scratch_shapes=[
            pltpu.VMEM(gate_re.shape, jnp.float32),
            pltpu.VMEM(gate_im.shape, jnp.float32),
            pltpu.SMEM(bit_orders.shape, jnp.int32),
            pltpu.SMEM(phase_pairs.shape, jnp.int32),
            pltpu.SMEM(phase_angles.shape, jnp.float32),
            pltpu.VMEM((CHUNKS, WIDE, 32, 128), jnp.float32),
            pltpu.VMEM((CHUNKS, WIDE, 32, 128), jnp.float32),
            pltpu.VMEM((4, 256, 128), jnp.float32),
            pltpu.VMEM((256, 512), jnp.float32),
            pltpu.VMEM((LAYERS, 512, 512), jnp.bfloat16),
            pltpu.VMEM((LAYERS, 512, 512), jnp.bfloat16),
            pltpu.VMEM((LAYERS, CHUNKS, 2, 8, 128), jnp.float32),
            pltpu.VMEM((LAYERS, CHUNKS, 2, 8, 128), jnp.float32),
            pltpu.SemaphoreType.DMA,
            pltpu.SemaphoreType.DMA((CHUNKS,)),
            pltpu.SemaphoreType.DMA,
            pltpu.SemaphoreType.DMA,
            pltpu.SemaphoreType.DMA((2 * CHUNKS,)),
            pltpu.SemaphoreType.DMA((6,)),
            pltpu.VMEM(given.shape, jnp.float32),
        ],
        compiler_params=pltpu.CompilerParams(
            collective_id=0, has_side_effects=True, vmem_limit_bytes=48 * 1024 * 1024
        ),
        cost_estimate=pl.CostEstimate(flops=4_831_838_208, bytes_accessed=4_194_304, transcendentals=49_152),
    )(*[pltpu.with_memory_space_constraint(x, pltpu.HBM) for x in operands])


def local(state, gate_re, gate_im, bit_orders, phase_pairs, phase_angles):
    given = state.reshape(2, 1024, 128).transpose(1, 0, 2).reshape(WIDE, CHUNKS, 32, 128)
    result = run(given, gate_re, gate_im, bit_orders, phase_pairs.transpose(0, 2, 1), phase_angles)
    return result.reshape(1024, 2, 128).transpose(1, 0, 2).reshape(state.shape)


def solution(mesh):
    return jax.shard_map(
        local,
        mesh=mesh,
        in_specs=(P(None, ("wide", "narrow")), P(), P(), P(), P(), P()),
        out_specs=P(None, ("wide", "narrow")),
        check_vma=False,
    )
```

```python
import jax
import jax.numpy as jnp
from jax import lax
from jax.experimental import pallas as pl
from jax.experimental.pallas import tpu as pltpu
from jax.sharding import PartitionSpec as P

LAYERS = 6
PHASES = 16
WIDE = 32
CHUNKS = 2


def dot_rows(left, right):
    return lax.dot_general(left, right, (((1,), (0,)), ((), ())), preferred_element_type=jnp.float32)


def split(values):
    high = values.astype(jnp.bfloat16)
    low = (values - high.astype(jnp.float32)).astype(jnp.bfloat16)
    return high, low


def transpose_granules(tiles):
    lane = lax.broadcasted_iota(jnp.int32, (8, 128), 1)
    skewed = [tiles[i] if i == 0 else pltpu.roll(tiles[i], 8 * i, 1) for i in range(16)]
    turned = [skewed[(-i) % 16] for i in range(16)]
    for bit in range(4):
        mask = (lane // (8 << bit)) % 2 == 1
        turned = [jnp.where(mask, turned[(i - (1 << bit)) % 16], turned[i]) for i in range(16)]
    return [turned[k] if k == 0 else pltpu.roll(turned[k], 128 - 8 * k, 1) for k in range(16)]


def partners(me):
    turns = [(1 - 2 * ((me // (1 << bit)) % 2)) * (1 << bit) for bit in range(5)]
    return [me + sum(turns[bit] for bit in range(5) if (distance >> bit) & 1) for distance in range(WIDE)]


def kernel(
    given,
    gate_re_given,
    gate_im_given,
    bit_orders_given,
    phase_pairs_given,
    phase_angles_given,
    result,
    gate_re,
    gate_im,
    bit_orders,
    phase_pairs,
    phase_angles,
    landed,
    leaving,
    held,
    product,
    weight_high,
    weight_low,
    cosines,
    sines,
    in_send,
    in_recv,
    out_send,
    out_recv,
    own_sem,
    fetch_sem,
    lines,
):
    me = lax.axis_index("wide")
    narrow = lax.axis_index("narrow")
    barrier = pltpu.get_barrier_semaphore()

    others = partners(me)
    swing = (me // 2) % 2
    turned = partners(me + swing * 4 * (1 - 2 * ((me // 4) % 2)))
    sequence = [turned[i] for i in range(WIDE - 1, 0, -1) if i != 4] + [others[4]]
    for distance in (24, 16, 8, 7, 6, 5, 4, 3, 2, 1):
        pl.semaphore_signal(
            barrier, inc=1, device_id={"wide": others[distance]}, device_id_type=pl.DeviceIdType.MESH
        )
    parameters = [
        pltpu.make_async_copy(source, target, fetch_sem.at[i])
        for i, (source, target) in enumerate(
            [
                (gate_re_given, gate_re),
                (gate_im_given, gate_im),
                (bit_orders_given, bit_orders),
                (phase_pairs_given, phase_pairs),
                (phase_angles_given, phase_angles),
            ]
        )
    ]
    pl.semaphore_wait(barrier, 10)
    for distance in (24, 16, 8):
        pl.semaphore_signal(
            lines, inc=1, device_id={"wide": others[distance]}, device_id_type=pl.DeviceIdType.MESH
        )

    def send_in(chunk, targets):
        for other in targets:
            pltpu.make_async_remote_copy(
                src_ref=given.at[other, chunk],
                dst_ref=landed.at[chunk, me],
                send_sem=in_send,
                recv_sem=in_recv.at[chunk],
                device_id={"wide": other},
                device_id_type=pl.DeviceIdType.MESH,
            ).start()

    send_in(0, sequence[24:])
    pl.semaphore_wait(lines, 3)
    send_in(0, sequence[:24])
    send_in(1, sequence)
    for chunk in range(CHUNKS):
        pltpu.make_async_copy(given.at[me, chunk], landed.at[chunk, me], own_sem.at[chunk]).start()

    for copy in parameters:
        copy.start()
    for copy in parameters:
        copy.wait()

    def build(layer, carry):
        gr_high, gr_low = split(gate_re[layer])
        gi_high, gi_low = split(gate_im[layer])
        lanes = lax.broadcasted_iota(jnp.int32, (128, 128), 1)
        rows = lax.broadcasted_iota(jnp.int32, (128, 128), 0)
        base = jnp.zeros((128, 128), jnp.int32)
        for which in range(7):
            base = base + jnp.left_shift(jnp.right_shift(lanes, which) & 1, bit_orders[layer, which])
        top = jnp.left_shift(jnp.int32(1), bit_orders[layer, 7])
        for h in range(2):
            for e in range(2):
                source = base + e * top
                picks = jnp.where(rows + h * 128 == source, 1.0, 0.0).astype(jnp.bfloat16)
                for store, re, im in ((weight_high, gr_high, gi_high), (weight_low, gr_low, gi_low)):
                    real = lax.dot_general(
                        picks, re, (((1,), (1,)), ((), ())), preferred_element_type=jnp.float32
                    ).astype(jnp.bfloat16)
                    imag = lax.dot_general(
                        picks, im, (((1,), (1,)), ((), ())), preferred_element_type=jnp.float32
                    ).astype(jnp.bfloat16)
                    store[layer, pl.ds(h * 256, 128), pl.ds(e * 256, 128)] = real
                    store[layer, pl.ds(h * 256, 128), pl.ds(e * 256 + 128, 128)] = imag
                    store[layer, pl.ds(h * 256 + 128, 128), pl.ds(e * 256, 128)] = -imag
                    store[layer, pl.ds(h * 256 + 128, 128), pl.ds(e * 256 + 128, 128)] = real
        return carry

    lax.fori_loop(0, LAYERS, build, 0)

    lane = lax.broadcasted_iota(jnp.int32, (8, 128), 1)
    sublane = lax.broadcasted_iota(jnp.int32, (8, 128), 0)

    def phases(layer, carry):
        odd = layer % 2
        middle = odd * sublane + (1 - odd) * narrow
        low = middle * 256 + lane
        for chunk in range(CHUNKS):
            for h in range(2):
                position = low + (chunk * 2048 + h * 128)
                phi = jnp.zeros((8, 128), jnp.float32)
                for gate in range(PHASES):
                    first = jnp.right_shift(position, phase_pairs[layer, 0, gate])
                    second = jnp.right_shift(position, phase_pairs[layer, 1, gate])
                    phi = phi + phase_angles[layer, gate] * (first & second & 1).astype(jnp.float32)
                cosines[layer, chunk, h] = jnp.cos(phi)
                sines[layer, chunk, h] = jnp.sin(phi)
        return carry

    lax.fori_loop(0, LAYERS, phases, 0)

    def one_chunk(chunk, carry):
        arrivals = landed.at[chunk, pl.ds(0, WIDE - 1)]
        pltpu.make_async_copy(arrivals, arrivals, in_recv.at[chunk]).wait()
        pltpu.make_async_copy(given.at[me, chunk], landed.at[chunk, me], own_sem.at[chunk]).wait()

        for a_high in range(2):
            for a2_high in range(2):
                for part in range(2):
                    rows = pl.ds(a2_high * 2 + part, 8, stride=4)
                    tiles = [landed[chunk, a_high * 16 + i, rows, :] for i in range(16)]
                    tiles = transpose_granules(tiles)
                    for i in range(16):
                        held[a_high * 2 + part, pl.ds((a2_high * 16 + i) * 8, 8), :] = tiles[i]

        for layer in range(LAYERS):
            x = jnp.concatenate([held[k] for k in range(4)], axis=1)
            high, low = split(x)
            w_high = weight_high[layer]
            w_low = weight_low[layer]
            product[...] = dot_rows(high, w_high) + (dot_rows(low, w_high) + dot_rows(high, w_low))
            for h in range(2):
                cosine = cosines[layer, chunk, h]
                sine = sines[layer, chunk, h]
                for s in range(2):
                    reals = []
                    imags = []
                    for i in range(16):
                        rows = pl.ds((s * 16 + i) * 8, 8)
                        re = product[rows, pl.ds(h * 256, 128)]
                        im = product[rows, pl.ds(h * 256 + 128, 128)]
                        reals.append(re * cosine - im * sine)
                        imags.append(re * sine + im * cosine)
                    if layer < LAYERS - 1:
                        reals = transpose_granules(reals)
                        imags = transpose_granules(imags)
                        for i in range(16):
                            rows = pl.ds((h * 16 + i) * 8, 8)
                            held[s * 2, rows, :] = reals[i]
                            held[s * 2 + 1, rows, :] = imags[i]
                    else:
                        for i in range(16):
                            leaving[chunk, s * 16 + i, pl.ds(h * 2, 8, stride=4), :] = reals[i]
                            leaving[chunk, s * 16 + i, pl.ds(h * 2 + 1, 8, stride=4), :] = imags[i]

        for other in sequence:
            pltpu.make_async_remote_copy(
                src_ref=leaving.at[chunk, other],
                dst_ref=result.at[me, chunk],
                send_sem=out_send,
                recv_sem=out_recv,
                device_id={"wide": other},
                device_id_type=pl.DeviceIdType.MESH,
            ).start()
        pltpu.make_async_copy(leaving.at[chunk, me], result.at[me, chunk], own_sem.at[CHUNKS + chunk]).start()
        return carry

    lax.fori_loop(0, CHUNKS, one_chunk, 0)

    sent = given.at[pl.ds(0, WIDE - 1)]
    pltpu.make_async_copy(sent, sent, in_send).wait()
    for chunk in range(CHUNKS):
        pltpu.make_async_copy(leaving.at[chunk, me], result.at[me, chunk], own_sem.at[CHUNKS + chunk]).wait()
    arrived = result.at[pl.ds(0, WIDE - 1)]
    pltpu.make_async_copy(arrived, arrived, out_recv).wait()
    pltpu.make_async_copy(arrived, arrived, out_send).wait()


def run(given, gate_re, gate_im, bit_orders, phase_pairs, phase_angles):
    operands = (given, gate_re, gate_im, bit_orders, phase_pairs, phase_angles)
    return pl.pallas_call(
        kernel,
        out_shape=pltpu.VMEM(given.shape, jnp.float32),
        in_specs=[pl.BlockSpec(memory_space=pltpu.HBM)] * len(operands),
        out_specs=pl.BlockSpec(memory_space=pltpu.VMEM),
        scratch_shapes=[
            pltpu.VMEM(gate_re.shape, jnp.float32),
            pltpu.VMEM(gate_im.shape, jnp.float32),
            pltpu.SMEM(bit_orders.shape, jnp.int32),
            pltpu.SMEM(phase_pairs.shape, jnp.int32),
            pltpu.SMEM(phase_angles.shape, jnp.float32),
            pltpu.VMEM((CHUNKS, WIDE, 32, 128), jnp.float32),
            pltpu.VMEM((CHUNKS, WIDE, 32, 128), jnp.float32),
            pltpu.VMEM((4, 256, 128), jnp.float32),
            pltpu.VMEM((256, 512), jnp.float32),
            pltpu.VMEM((LAYERS, 512, 512), jnp.bfloat16),
            pltpu.VMEM((LAYERS, 512, 512), jnp.bfloat16),
            pltpu.VMEM((LAYERS, CHUNKS, 2, 8, 128), jnp.float32),
            pltpu.VMEM((LAYERS, CHUNKS, 2, 8, 128), jnp.float32),
            pltpu.SemaphoreType.DMA,
            pltpu.SemaphoreType.DMA((CHUNKS,)),
            pltpu.SemaphoreType.DMA,
            pltpu.SemaphoreType.DMA,
            pltpu.SemaphoreType.DMA((2 * CHUNKS,)),
            pltpu.SemaphoreType.DMA((5,)),
            pltpu.SemaphoreType.REGULAR,
        ],
        compiler_params=pltpu.CompilerParams(
            collective_id=0, has_side_effects=True, vmem_limit_bytes=48 * 1024 * 1024
        ),
        cost_estimate=pl.CostEstimate(flops=4_831_838_208, bytes_accessed=4_194_304, transcendentals=49_152),
    )(*[pltpu.with_memory_space_constraint(x, pltpu.HBM) for x in operands])


def local(state, gate_re, gate_im, bit_orders, phase_pairs, phase_angles):
    given = state.reshape(2, 1024, 128).transpose(1, 0, 2).reshape(WIDE, CHUNKS, 32, 128)
    result = run(given, gate_re, gate_im, bit_orders, phase_pairs.transpose(0, 2, 1), phase_angles)
    return result.reshape(1024, 2, 128).transpose(1, 0, 2).reshape(state.shape)


def solution(mesh):
    return jax.shard_map(
        local,
        mesh=mesh,
        in_specs=(P(None, ("wide", "narrow")), P(), P(), P(), P(), P()),
        out_specs=P(None, ("wide", "narrow")),
        check_vma=False,
    )
```

```python
import jax
import jax.numpy as jnp
from jax import lax
from jax.experimental import pallas as pl
from jax.experimental.pallas import tpu as pltpu
from jax.sharding import PartitionSpec as P

LAYERS = 6
PHASES = 16
WIDE = 32
CHUNKS = 2


def dot_rows(left, right):
    return lax.dot_general(left, right, (((1,), (0,)), ((), ())), preferred_element_type=jnp.float32)


def split(values):
    high = values.astype(jnp.bfloat16)
    low = (values - high.astype(jnp.float32)).astype(jnp.bfloat16)
    return high, low


def transpose_granules(tiles):
    lane = lax.broadcasted_iota(jnp.int32, (8, 128), 1)
    skewed = [tiles[i] if i == 0 else pltpu.roll(tiles[i], 8 * i, 1) for i in range(16)]
    turned = [skewed[(-i) % 16] for i in range(16)]
    for bit in range(4):
        mask = (lane // (8 << bit)) % 2 == 1
        turned = [jnp.where(mask, turned[(i - (1 << bit)) % 16], turned[i]) for i in range(16)]
    return [turned[k] if k == 0 else pltpu.roll(turned[k], 128 - 8 * k, 1) for k in range(16)]


def partners(me):
    turns = [(1 - 2 * ((me // (1 << bit)) % 2)) * (1 << bit) for bit in range(5)]
    return [me + sum(turns[bit] for bit in range(5) if (distance >> bit) & 1) for distance in range(WIDE)]


def kernel(
    given,
    gate_re_given,
    gate_im_given,
    bit_orders_given,
    phase_pairs_given,
    phase_angles_given,
    result,
    gate_re,
    gate_im,
    bit_orders,
    phase_pairs,
    phase_angles,
    landed,
    leaving,
    held,
    product,
    weight_high,
    weight_low,
    cosines,
    sines,
    in_send,
    in_recv,
    out_send,
    out_recv,
    own_sem,
    fetch_sem,
    lines,
):
    me = lax.axis_index("wide")
    narrow = lax.axis_index("narrow")
    barrier = pltpu.get_barrier_semaphore()

    others = partners(me)
    swing = (me // 2) % 2
    turned = partners(me + swing * 4 * (1 - 2 * ((me // 4) % 2)))
    sequence = [turned[i] for i in range(WIDE - 1, 0, -1) if i != 4] + [others[4]]
    for distance in (24, 16, 8, 7, 6, 5, 4, 3, 2, 1):
        pl.semaphore_signal(
            barrier, inc=1, device_id={"wide": others[distance]}, device_id_type=pl.DeviceIdType.MESH
        )
    parameters = [
        pltpu.make_async_copy(source, target, fetch_sem.at[i])
        for i, (source, target) in enumerate(
            [
                (gate_re_given, gate_re),
                (gate_im_given, gate_im),
                (bit_orders_given, bit_orders),
                (phase_pairs_given, phase_pairs),
                (phase_angles_given, phase_angles),
            ]
        )
    ]
    pl.semaphore_wait(barrier, 10)
    for line, distance in enumerate((8, 16, 24)):
        pl.semaphore_signal(
            lines.at[line], inc=1, device_id={"wide": others[distance]}, device_id_type=pl.DeviceIdType.MESH
        )

    def send_in(chunk, targets):
        for other in targets:
            pltpu.make_async_remote_copy(
                src_ref=given.at[other, chunk],
                dst_ref=landed.at[chunk, me],
                send_sem=in_send,
                recv_sem=in_recv.at[chunk],
                device_id={"wide": other},
                device_id_type=pl.DeviceIdType.MESH,
            ).start()

    send_in(0, sequence[24:])
    for line in range(3):
        pl.semaphore_wait(lines.at[line], 1)
        send_in(0, sequence[16 - 8 * line : 24 - 8 * line])
    send_in(1, sequence[:8] + sequence[24:] + sequence[8:24])
    for chunk in range(CHUNKS):
        pltpu.make_async_copy(given.at[me, chunk], landed.at[chunk, me], own_sem.at[chunk]).start()

    for copy in parameters:
        copy.start()
    for copy in parameters:
        copy.wait()

    def build(layer, carry):
        gr_high, gr_low = split(gate_re[layer])
        gi_high, gi_low = split(gate_im[layer])
        lanes = lax.broadcasted_iota(jnp.int32, (128, 128), 1)
        rows = lax.broadcasted_iota(jnp.int32, (128, 128), 0)
        base = jnp.zeros((128, 128), jnp.int32)
        for which in range(7):
            base = base + jnp.left_shift(jnp.right_shift(lanes, which) & 1, bit_orders[layer, which])
        top = jnp.left_shift(jnp.int32(1), bit_orders[layer, 7])
        for h in range(2):
            for e in range(2):
                source = base + e * top
                picks = jnp.where(rows + h * 128 == source, 1.0, 0.0).astype(jnp.bfloat16)
                for store, re, im in ((weight_high, gr_high, gi_high), (weight_low, gr_low, gi_low)):
                    real = lax.dot_general(
                        picks, re, (((1,), (1,)), ((), ())), preferred_element_type=jnp.float32
                    ).astype(jnp.bfloat16)
                    imag = lax.dot_general(
                        picks, im, (((1,), (1,)), ((), ())), preferred_element_type=jnp.float32
                    ).astype(jnp.bfloat16)
                    store[layer, pl.ds(h * 256, 128), pl.ds(e * 256, 128)] = real
                    store[layer, pl.ds(h * 256, 128), pl.ds(e * 256 + 128, 128)] = imag
                    store[layer, pl.ds(h * 256 + 128, 128), pl.ds(e * 256, 128)] = -imag
                    store[layer, pl.ds(h * 256 + 128, 128), pl.ds(e * 256 + 128, 128)] = real
        return carry

    lax.fori_loop(0, LAYERS, build, 0)

    lane = lax.broadcasted_iota(jnp.int32, (8, 128), 1)
    sublane = lax.broadcasted_iota(jnp.int32, (8, 128), 0)

    def phases(layer, carry):
        odd = layer % 2
        middle = odd * sublane + (1 - odd) * narrow
        low = middle * 256 + lane
        for chunk in range(CHUNKS):
            for h in range(2):
                position = low + (chunk * 2048 + h * 128)
                phi = jnp.zeros((8, 128), jnp.float32)
                for gate in range(PHASES):
                    first = jnp.right_shift(position, phase_pairs[layer, 0, gate])
                    second = jnp.right_shift(position, phase_pairs[layer, 1, gate])
                    phi = phi + phase_angles[layer, gate] * (first & second & 1).astype(jnp.float32)
                cosines[layer, chunk, h] = jnp.cos(phi)
                sines[layer, chunk, h] = jnp.sin(phi)
        return carry

    lax.fori_loop(0, LAYERS, phases, 0)

    def one_chunk(chunk, carry):
        arrivals = landed.at[chunk, pl.ds(0, WIDE - 1)]
        pltpu.make_async_copy(arrivals, arrivals, in_recv.at[chunk]).wait()
        pltpu.make_async_copy(given.at[me, chunk], landed.at[chunk, me], own_sem.at[chunk]).wait()

        for a_high in range(2):
            for a2_high in range(2):
                for part in range(2):
                    rows = pl.ds(a2_high * 2 + part, 8, stride=4)
                    tiles = [landed[chunk, a_high * 16 + i, rows, :] for i in range(16)]
                    tiles = transpose_granules(tiles)
                    for i in range(16):
                        held[a_high * 2 + part, pl.ds((a2_high * 16 + i) * 8, 8), :] = tiles[i]

        for layer in range(LAYERS):
            x = jnp.concatenate([held[k] for k in range(4)], axis=1)
            high, low = split(x)
            w_high = weight_high[layer]
            w_low = weight_low[layer]
            product[...] = dot_rows(high, w_high) + (dot_rows(low, w_high) + dot_rows(high, w_low))
            for h in range(2):
                cosine = cosines[layer, chunk, h]
                sine = sines[layer, chunk, h]
                for s in range(2):
                    reals = []
                    imags = []
                    for i in range(16):
                        rows = pl.ds((s * 16 + i) * 8, 8)
                        re = product[rows, pl.ds(h * 256, 128)]
                        im = product[rows, pl.ds(h * 256 + 128, 128)]
                        reals.append(re * cosine - im * sine)
                        imags.append(re * sine + im * cosine)
                    if layer < LAYERS - 1:
                        reals = transpose_granules(reals)
                        imags = transpose_granules(imags)
                        for i in range(16):
                            rows = pl.ds((h * 16 + i) * 8, 8)
                            held[s * 2, rows, :] = reals[i]
                            held[s * 2 + 1, rows, :] = imags[i]
                    else:
                        for i in range(16):
                            leaving[chunk, s * 16 + i, pl.ds(h * 2, 8, stride=4), :] = reals[i]
                            leaving[chunk, s * 16 + i, pl.ds(h * 2 + 1, 8, stride=4), :] = imags[i]

        for other in sequence:
            pltpu.make_async_remote_copy(
                src_ref=leaving.at[chunk, other],
                dst_ref=result.at[me, chunk],
                send_sem=out_send,
                recv_sem=out_recv,
                device_id={"wide": other},
                device_id_type=pl.DeviceIdType.MESH,
            ).start()
        pltpu.make_async_copy(leaving.at[chunk, me], result.at[me, chunk], own_sem.at[CHUNKS + chunk]).start()
        return carry

    lax.fori_loop(0, CHUNKS, one_chunk, 0)

    sent = given.at[pl.ds(0, WIDE - 1)]
    pltpu.make_async_copy(sent, sent, in_send).wait()
    for chunk in range(CHUNKS):
        pltpu.make_async_copy(leaving.at[chunk, me], result.at[me, chunk], own_sem.at[CHUNKS + chunk]).wait()
    arrived = result.at[pl.ds(0, WIDE - 1)]
    pltpu.make_async_copy(arrived, arrived, out_recv).wait()
    pltpu.make_async_copy(arrived, arrived, out_send).wait()


def run(given, gate_re, gate_im, bit_orders, phase_pairs, phase_angles):
    operands = (given, gate_re, gate_im, bit_orders, phase_pairs, phase_angles)
    return pl.pallas_call(
        kernel,
        out_shape=pltpu.VMEM(given.shape, jnp.float32),
        in_specs=[pl.BlockSpec(memory_space=pltpu.HBM)] * len(operands),
        out_specs=pl.BlockSpec(memory_space=pltpu.VMEM),
        scratch_shapes=[
            pltpu.VMEM(gate_re.shape, jnp.float32),
            pltpu.VMEM(gate_im.shape, jnp.float32),
            pltpu.SMEM(bit_orders.shape, jnp.int32),
            pltpu.SMEM(phase_pairs.shape, jnp.int32),
            pltpu.SMEM(phase_angles.shape, jnp.float32),
            pltpu.VMEM((CHUNKS, WIDE, 32, 128), jnp.float32),
            pltpu.VMEM((CHUNKS, WIDE, 32, 128), jnp.float32),
            pltpu.VMEM((4, 256, 128), jnp.float32),
            pltpu.VMEM((256, 512), jnp.float32),
            pltpu.VMEM((LAYERS, 512, 512), jnp.bfloat16),
            pltpu.VMEM((LAYERS, 512, 512), jnp.bfloat16),
            pltpu.VMEM((LAYERS, CHUNKS, 2, 8, 128), jnp.float32),
            pltpu.VMEM((LAYERS, CHUNKS, 2, 8, 128), jnp.float32),
            pltpu.SemaphoreType.DMA,
            pltpu.SemaphoreType.DMA((CHUNKS,)),
            pltpu.SemaphoreType.DMA,
            pltpu.SemaphoreType.DMA,
            pltpu.SemaphoreType.DMA((2 * CHUNKS,)),
            pltpu.SemaphoreType.DMA((5,)),
            pltpu.SemaphoreType.REGULAR((3,)),
        ],
        compiler_params=pltpu.CompilerParams(
            collective_id=0, has_side_effects=True, vmem_limit_bytes=48 * 1024 * 1024
        ),
        cost_estimate=pl.CostEstimate(flops=4_831_838_208, bytes_accessed=4_194_304, transcendentals=49_152),
    )(*[pltpu.with_memory_space_constraint(x, pltpu.HBM) for x in operands])


def local(state, gate_re, gate_im, bit_orders, phase_pairs, phase_angles):
    given = state.reshape(2, 1024, 128).transpose(1, 0, 2).reshape(WIDE, CHUNKS, 32, 128)
    result = run(given, gate_re, gate_im, bit_orders, phase_pairs.transpose(0, 2, 1), phase_angles)
    return result.reshape(1024, 2, 128).transpose(1, 0, 2).reshape(state.shape)


def solution(mesh):
    return jax.shard_map(
        local,
        mesh=mesh,
        in_specs=(P(None, ("wide", "narrow")), P(), P(), P(), P(), P()),
        out_specs=P(None, ("wide", "narrow")),
        check_vma=False,
    )
```

```python
import jax
import jax.numpy as jnp
from jax import lax
from jax.experimental import pallas as pl
from jax.experimental.pallas import tpu as pltpu
from jax.sharding import PartitionSpec as P

LAYERS = 6
PHASES = 16
WIDE = 32
CHUNKS = 2


def dot_rows(left, right):
    return lax.dot_general(left, right, (((1,), (0,)), ((), ())), preferred_element_type=jnp.float32)


def split(values):
    high = values.astype(jnp.bfloat16)
    low = (values - high.astype(jnp.float32)).astype(jnp.bfloat16)
    return high, low


def transpose_granules(tiles):
    lane = lax.broadcasted_iota(jnp.int32, (8, 128), 1)
    skewed = [tiles[i] if i == 0 else pltpu.roll(tiles[i], 8 * i, 1) for i in range(16)]
    turned = [skewed[(-i) % 16] for i in range(16)]
    for bit in range(4):
        mask = (lane // (8 << bit)) % 2 == 1
        turned = [jnp.where(mask, turned[(i - (1 << bit)) % 16], turned[i]) for i in range(16)]
    return [turned[k] if k == 0 else pltpu.roll(turned[k], 128 - 8 * k, 1) for k in range(16)]


def partners(me):
    turns = [(1 - 2 * ((me // (1 << bit)) % 2)) * (1 << bit) for bit in range(5)]
    return [me + sum(turns[bit] for bit in range(5) if (distance >> bit) & 1) for distance in range(WIDE)]


def kernel(
    given,
    gate_re_given,
    gate_im_given,
    bit_orders_given,
    phase_pairs_given,
    phase_angles_given,
    result,
    gate_re,
    gate_im,
    bit_orders,
    phase_pairs,
    phase_angles,
    landed,
    leaving,
    held,
    product,
    weight_high,
    weight_low,
    cosines,
    sines,
    in_send,
    in_recv,
    out_send,
    out_recv,
    own_sem,
    fetch_sem,
    lines,
):
    me = lax.axis_index("wide")
    narrow = lax.axis_index("narrow")
    barrier = pltpu.get_barrier_semaphore()

    others = partners(me)
    swing = (me // 2) % 2
    turned = partners(me + swing * 4 * (1 - 2 * ((me // 4) % 2)))
    sequence = [turned[i] for i in range(WIDE - 1, 0, -1) if i != 4] + [others[4]]
    for distance in (24, 16, 8, 7, 6, 5, 4, 3, 2, 1):
        pl.semaphore_signal(
            barrier, inc=1, device_id={"wide": others[distance]}, device_id_type=pl.DeviceIdType.MESH
        )
    parameters = [
        pltpu.make_async_copy(source, target, fetch_sem.at[i])
        for i, (source, target) in enumerate(
            [
                (gate_re_given, gate_re),
                (gate_im_given, gate_im),
                (bit_orders_given, bit_orders),
                (phase_pairs_given, phase_pairs),
                (phase_angles_given, phase_angles),
            ]
        )
    ]
    pl.semaphore_wait(barrier, 10)
    for line, distance in enumerate((8, 16, 24)):
        pl.semaphore_signal(
            lines.at[line], inc=1, device_id={"wide": others[distance]}, device_id_type=pl.DeviceIdType.MESH
        )

    def send_in(chunk, targets):
        for other in targets:
            pltpu.make_async_remote_copy(
                src_ref=given.at[other, chunk],
                dst_ref=landed.at[chunk, me],
                send_sem=in_send,
                recv_sem=in_recv.at[chunk],
                device_id={"wide": other},
                device_id_type=pl.DeviceIdType.MESH,
            ).start()

    send_in(0, [others[distance] for distance in (7, 6, 5, 4, 3, 2, 1)])
    for line in range(3):
        pl.semaphore_wait(lines.at[line], 1)
        send_in(0, sequence[16 - 8 * line : 24 - 8 * line])
    send_in(1, sequence[:8] + sequence[24:] + sequence[8:24])
    for chunk in range(CHUNKS):
        pltpu.make_async_copy(given.at[me, chunk], landed.at[chunk, me], own_sem.at[chunk]).start()

    for copy in parameters:
        copy.start()
    for copy in parameters:
        copy.wait()

    def build(layer, carry):
        gr_high, gr_low = split(gate_re[layer])
        gi_high, gi_low = split(gate_im[layer])
        lanes = lax.broadcasted_iota(jnp.int32, (128, 128), 1)
        rows = lax.broadcasted_iota(jnp.int32, (128, 128), 0)
        base = jnp.zeros((128, 128), jnp.int32)
        for which in range(7):
            base = base + jnp.left_shift(jnp.right_shift(lanes, which) & 1, bit_orders[layer, which])
        top = jnp.left_shift(jnp.int32(1), bit_orders[layer, 7])
        for h in range(2):
            for e in range(2):
                source = base + e * top
                picks = jnp.where(rows + h * 128 == source, 1.0, 0.0).astype(jnp.bfloat16)
                for store, re, im in ((weight_high, gr_high, gi_high), (weight_low, gr_low, gi_low)):
                    real = lax.dot_general(
                        picks, re, (((1,), (1,)), ((), ())), preferred_element_type=jnp.float32
                    ).astype(jnp.bfloat16)
                    imag = lax.dot_general(
                        picks, im, (((1,), (1,)), ((), ())), preferred_element_type=jnp.float32
                    ).astype(jnp.bfloat16)
                    store[layer, pl.ds(h * 256, 128), pl.ds(e * 256, 128)] = real
                    store[layer, pl.ds(h * 256, 128), pl.ds(e * 256 + 128, 128)] = imag
                    store[layer, pl.ds(h * 256 + 128, 128), pl.ds(e * 256, 128)] = -imag
                    store[layer, pl.ds(h * 256 + 128, 128), pl.ds(e * 256 + 128, 128)] = real
        return carry

    lax.fori_loop(0, LAYERS, build, 0)

    lane = lax.broadcasted_iota(jnp.int32, (8, 128), 1)
    sublane = lax.broadcasted_iota(jnp.int32, (8, 128), 0)

    def phases(layer, carry):
        odd = layer % 2
        middle = odd * sublane + (1 - odd) * narrow
        low = middle * 256 + lane
        for chunk in range(CHUNKS):
            for h in range(2):
                position = low + (chunk * 2048 + h * 128)
                phi = jnp.zeros((8, 128), jnp.float32)
                for gate in range(PHASES):
                    first = jnp.right_shift(position, phase_pairs[layer, 0, gate])
                    second = jnp.right_shift(position, phase_pairs[layer, 1, gate])
                    phi = phi + phase_angles[layer, gate] * (first & second & 1).astype(jnp.float32)
                cosines[layer, chunk, h] = jnp.cos(phi)
                sines[layer, chunk, h] = jnp.sin(phi)
        return carry

    lax.fori_loop(0, LAYERS, phases, 0)

    def one_chunk(chunk, carry):
        arrivals = landed.at[chunk, pl.ds(0, WIDE - 1)]
        pltpu.make_async_copy(arrivals, arrivals, in_recv.at[chunk]).wait()
        pltpu.make_async_copy(given.at[me, chunk], landed.at[chunk, me], own_sem.at[chunk]).wait()

        for a_high in range(2):
            for a2_high in range(2):
                for part in range(2):
                    rows = pl.ds(a2_high * 2 + part, 8, stride=4)
                    tiles = [landed[chunk, a_high * 16 + i, rows, :] for i in range(16)]
                    tiles = transpose_granules(tiles)
                    for i in range(16):
                        held[a_high * 2 + part, pl.ds((a2_high * 16 + i) * 8, 8), :] = tiles[i]

        for layer in range(LAYERS):
            x = jnp.concatenate([held[k] for k in range(4)], axis=1)
            high, low = split(x)
            w_high = weight_high[layer]
            w_low = weight_low[layer]
            product[...] = dot_rows(high, w_high) + (dot_rows(low, w_high) + dot_rows(high, w_low))
            for h in range(2):
                cosine = cosines[layer, chunk, h]
                sine = sines[layer, chunk, h]
                for s in range(2):
                    reals = []
                    imags = []
                    for i in range(16):
                        rows = pl.ds((s * 16 + i) * 8, 8)
                        re = product[rows, pl.ds(h * 256, 128)]
                        im = product[rows, pl.ds(h * 256 + 128, 128)]
                        reals.append(re * cosine - im * sine)
                        imags.append(re * sine + im * cosine)
                    if layer < LAYERS - 1:
                        reals = transpose_granules(reals)
                        imags = transpose_granules(imags)
                        for i in range(16):
                            rows = pl.ds((h * 16 + i) * 8, 8)
                            held[s * 2, rows, :] = reals[i]
                            held[s * 2 + 1, rows, :] = imags[i]
                    else:
                        for i in range(16):
                            leaving[chunk, s * 16 + i, pl.ds(h * 2, 8, stride=4), :] = reals[i]
                            leaving[chunk, s * 16 + i, pl.ds(h * 2 + 1, 8, stride=4), :] = imags[i]

        for other in sequence:
            pltpu.make_async_remote_copy(
                src_ref=leaving.at[chunk, other],
                dst_ref=result.at[me, chunk],
                send_sem=out_send,
                recv_sem=out_recv,
                device_id={"wide": other},
                device_id_type=pl.DeviceIdType.MESH,
            ).start()
        pltpu.make_async_copy(leaving.at[chunk, me], result.at[me, chunk], own_sem.at[CHUNKS + chunk]).start()
        return carry

    lax.fori_loop(0, CHUNKS, one_chunk, 0)

    sent = given.at[pl.ds(0, WIDE - 1)]
    pltpu.make_async_copy(sent, sent, in_send).wait()
    for chunk in range(CHUNKS):
        pltpu.make_async_copy(leaving.at[chunk, me], result.at[me, chunk], own_sem.at[CHUNKS + chunk]).wait()
    arrived = result.at[pl.ds(0, WIDE - 1)]
    pltpu.make_async_copy(arrived, arrived, out_recv).wait()
    pltpu.make_async_copy(arrived, arrived, out_send).wait()


def run(given, gate_re, gate_im, bit_orders, phase_pairs, phase_angles):
    operands = (given, gate_re, gate_im, bit_orders, phase_pairs, phase_angles)
    return pl.pallas_call(
        kernel,
        out_shape=pltpu.VMEM(given.shape, jnp.float32),
        in_specs=[pl.BlockSpec(memory_space=pltpu.HBM)] * len(operands),
        out_specs=pl.BlockSpec(memory_space=pltpu.VMEM),
        scratch_shapes=[
            pltpu.VMEM(gate_re.shape, jnp.float32),
            pltpu.VMEM(gate_im.shape, jnp.float32),
            pltpu.SMEM(bit_orders.shape, jnp.int32),
            pltpu.SMEM(phase_pairs.shape, jnp.int32),
            pltpu.SMEM(phase_angles.shape, jnp.float32),
            pltpu.VMEM((CHUNKS, WIDE, 32, 128), jnp.float32),
            pltpu.VMEM((CHUNKS, WIDE, 32, 128), jnp.float32),
            pltpu.VMEM((4, 256, 128), jnp.float32),
            pltpu.VMEM((256, 512), jnp.float32),
            pltpu.VMEM((LAYERS, 512, 512), jnp.bfloat16),
            pltpu.VMEM((LAYERS, 512, 512), jnp.bfloat16),
            pltpu.VMEM((LAYERS, CHUNKS, 2, 8, 128), jnp.float32),
            pltpu.VMEM((LAYERS, CHUNKS, 2, 8, 128), jnp.float32),
            pltpu.SemaphoreType.DMA,
            pltpu.SemaphoreType.DMA((CHUNKS,)),
            pltpu.SemaphoreType.DMA,
            pltpu.SemaphoreType.DMA,
            pltpu.SemaphoreType.DMA((2 * CHUNKS,)),
            pltpu.SemaphoreType.DMA((5,)),
            pltpu.SemaphoreType.REGULAR((3,)),
        ],
        compiler_params=pltpu.CompilerParams(
            collective_id=0, has_side_effects=True, vmem_limit_bytes=48 * 1024 * 1024
        ),
        cost_estimate=pl.CostEstimate(flops=4_831_838_208, bytes_accessed=4_194_304, transcendentals=49_152),
    )(*[pltpu.with_memory_space_constraint(x, pltpu.HBM) for x in operands])


def local(state, gate_re, gate_im, bit_orders, phase_pairs, phase_angles):
    given = state.reshape(2, 1024, 128).transpose(1, 0, 2).reshape(WIDE, CHUNKS, 32, 128)
    result = run(given, gate_re, gate_im, bit_orders, phase_pairs.transpose(0, 2, 1), phase_angles)
    return result.reshape(1024, 2, 128).transpose(1, 0, 2).reshape(state.shape)


def solution(mesh):
    return jax.shard_map(
        local,
        mesh=mesh,
        in_specs=(P(None, ("wide", "narrow")), P(), P(), P(), P(), P()),
        out_specs=P(None, ("wide", "narrow")),
        check_vma=False,
    )
```

```python
import jax
import jax.numpy as jnp
from jax import lax
from jax.experimental import pallas as pl
from jax.experimental.pallas import tpu as pltpu
from jax.sharding import PartitionSpec as P

LAYERS = 6
PHASES = 16
WIDE = 32
CHUNKS = 2


def dot_rows(left, right):
    return lax.dot_general(left, right, (((1,), (0,)), ((), ())), preferred_element_type=jnp.float32)


def split(values):
    high = values.astype(jnp.bfloat16)
    low = (values - high.astype(jnp.float32)).astype(jnp.bfloat16)
    return high, low


def transpose_granules(tiles):
    lane = lax.broadcasted_iota(jnp.int32, (8, 128), 1)
    skewed = [tiles[i] if i == 0 else pltpu.roll(tiles[i], 8 * i, 1) for i in range(16)]
    turned = [skewed[(-i) % 16] for i in range(16)]
    for bit in range(4):
        mask = (lane // (8 << bit)) % 2 == 1
        turned = [jnp.where(mask, turned[(i - (1 << bit)) % 16], turned[i]) for i in range(16)]
    return [turned[k] if k == 0 else pltpu.roll(turned[k], 128 - 8 * k, 1) for k in range(16)]


def partners(me):
    turns = [(1 - 2 * ((me // (1 << bit)) % 2)) * (1 << bit) for bit in range(5)]
    return [me + sum(turns[bit] for bit in range(5) if (distance >> bit) & 1) for distance in range(WIDE)]


def kernel(
    given,
    gate_re_given,
    gate_im_given,
    bit_orders_given,
    phase_pairs_given,
    phase_angles_given,
    result,
    gate_re,
    gate_im,
    bit_orders,
    phase_pairs,
    phase_angles,
    landed,
    leaving,
    held,
    product,
    weight_high,
    weight_low,
    cosines,
    sines,
    in_send,
    in_recv,
    out_send,
    out_recv,
    own_sem,
    fetch_sem,
    lines,
):
    me = lax.axis_index("wide")
    narrow = lax.axis_index("narrow")
    barrier = pltpu.get_barrier_semaphore()

    others = partners(me)
    swing = (me // 2) % 2
    turned = partners(me + swing * 4 * (1 - 2 * ((me // 4) % 2)))
    sequence = [turned[i] for i in range(WIDE - 1, 0, -1) if i != 4] + [others[4]]
    for distance in (24, 16, 8, 7, 6, 5, 4, 3, 2, 1):
        pl.semaphore_signal(
            barrier, inc=1, device_id={"wide": others[distance]}, device_id_type=pl.DeviceIdType.MESH
        )
    parameters = [
        pltpu.make_async_copy(source, target, fetch_sem.at[i])
        for i, (source, target) in enumerate(
            [
                (gate_re_given, gate_re),
                (gate_im_given, gate_im),
                (bit_orders_given, bit_orders),
                (phase_pairs_given, phase_pairs),
                (phase_angles_given, phase_angles),
            ]
        )
    ]
    pl.semaphore_wait(barrier, 10)
    for line, distance in enumerate((8, 16, 24)):
        pl.semaphore_signal(
            lines.at[line], inc=1, device_id={"wide": others[distance]}, device_id_type=pl.DeviceIdType.MESH
        )

    def send_in(chunk, targets):
        for other in targets:
            pltpu.make_async_remote_copy(
                src_ref=given.at[other, chunk],
                dst_ref=landed.at[chunk, me],
                send_sem=in_send,
                recv_sem=in_recv.at[chunk],
                device_id={"wide": other},
                device_id_type=pl.DeviceIdType.MESH,
            ).start()

    send_in(0, [others[distance] for distance in (7, 6, 5, 4, 3, 2, 1)])
    for line in range(3):
        pl.semaphore_wait(lines.at[line], 1)
        send_in(0, sequence[16 - 8 * line : 24 - 8 * line])
    send_in(1, sequence[:8] + sequence[24:] + sequence[8:24])
    for chunk in range(CHUNKS):
        pltpu.make_async_copy(given.at[me, chunk], landed.at[chunk, me], own_sem.at[chunk]).start()

    for copy in parameters:
        copy.start()
    for copy in parameters:
        copy.wait()

    def build(layer, carry):
        gr_high, gr_low = split(gate_re[layer])
        gi_high, gi_low = split(gate_im[layer])
        lanes = lax.broadcasted_iota(jnp.int32, (128, 128), 1)
        rows = lax.broadcasted_iota(jnp.int32, (128, 128), 0)
        base = jnp.zeros((128, 128), jnp.int32)
        for which in range(7):
            base = base + jnp.left_shift(jnp.right_shift(lanes, which) & 1, bit_orders[layer, which])
        top = jnp.left_shift(jnp.int32(1), bit_orders[layer, 7])
        for h in range(2):
            for e in range(2):
                source = base + e * top
                picks = jnp.where(rows + h * 128 == source, 1.0, 0.0).astype(jnp.bfloat16)
                for store, re, im in ((weight_high, gr_high, gi_high), (weight_low, gr_low, gi_low)):
                    real = lax.dot_general(
                        picks, re, (((1,), (1,)), ((), ())), preferred_element_type=jnp.float32
                    ).astype(jnp.bfloat16)
                    imag = lax.dot_general(
                        picks, im, (((1,), (1,)), ((), ())), preferred_element_type=jnp.float32
                    ).astype(jnp.bfloat16)
                    store[layer, pl.ds(h * 256, 128), pl.ds(e * 256, 128)] = real
                    store[layer, pl.ds(h * 256, 128), pl.ds(e * 256 + 128, 128)] = imag
                    store[layer, pl.ds(h * 256 + 128, 128), pl.ds(e * 256, 128)] = -imag
                    store[layer, pl.ds(h * 256 + 128, 128), pl.ds(e * 256 + 128, 128)] = real
        return carry

    lax.fori_loop(0, LAYERS, build, 0)

    lane = lax.broadcasted_iota(jnp.int32, (8, 128), 1)
    sublane = lax.broadcasted_iota(jnp.int32, (8, 128), 0)

    def phases(layer, carry):
        odd = layer % 2
        middle = odd * sublane + (1 - odd) * narrow
        low = middle * 256 + lane
        for chunk in range(CHUNKS):
            for h in range(2):
                position = low + (chunk * 2048 + h * 128)
                phi = jnp.zeros((8, 128), jnp.float32)
                for gate in range(PHASES):
                    first = jnp.right_shift(position, phase_pairs[layer, 0, gate])
                    second = jnp.right_shift(position, phase_pairs[layer, 1, gate])
                    phi = phi + phase_angles[layer, gate] * (first & second & 1).astype(jnp.float32)
                cosines[layer, chunk, h] = jnp.cos(phi)
                sines[layer, chunk, h] = jnp.sin(phi)
        return carry

    lax.fori_loop(0, LAYERS, phases, 0)

    def one_chunk(chunk, carry):
        arrivals = landed.at[chunk, pl.ds(0, WIDE - 1)]
        pltpu.make_async_copy(arrivals, arrivals, in_recv.at[chunk]).wait()
        pltpu.make_async_copy(given.at[me, chunk], landed.at[chunk, me], own_sem.at[chunk]).wait()

        for a_high in range(2):
            for a2_high in range(2):
                for part in range(2):
                    rows = pl.ds(a2_high * 2 + part, 8, stride=4)
                    tiles = [landed[chunk, a_high * 16 + i, rows, :] for i in range(16)]
                    tiles = transpose_granules(tiles)
                    for i in range(16):
                        held[a_high * 2 + part, pl.ds((a2_high * 16 + i) * 8, 8), :] = tiles[i]

        for layer in range(LAYERS):
            x = jnp.concatenate([held[k] for k in range(4)], axis=1)
            high, low = split(x)
            w_high = weight_high[layer]
            w_low = weight_low[layer]
            product[...] = dot_rows(high, w_high) + (dot_rows(low, w_high) + dot_rows(high, w_low))
            for h in range(2):
                cosine = cosines[layer, chunk, h]
                sine = sines[layer, chunk, h]
                for s in range(2):
                    reals = []
                    imags = []
                    for i in range(16):
                        rows = pl.ds((s * 16 + i) * 8, 8)
                        re = product[rows, pl.ds(h * 256, 128)]
                        im = product[rows, pl.ds(h * 256 + 128, 128)]
                        reals.append(re * cosine - im * sine)
                        imags.append(re * sine + im * cosine)
                    if layer < LAYERS - 1:
                        reals = transpose_granules(reals)
                        imags = transpose_granules(imags)
                        for i in range(16):
                            rows = pl.ds((h * 16 + i) * 8, 8)
                            held[s * 2, rows, :] = reals[i]
                            held[s * 2 + 1, rows, :] = imags[i]
                    else:
                        for i in range(16):
                            leaving[chunk, s * 16 + i, pl.ds(h * 2, 8, stride=4), :] = reals[i]
                            leaving[chunk, s * 16 + i, pl.ds(h * 2 + 1, 8, stride=4), :] = imags[i]

        for other in sequence[:27] + [others[4]] + sequence[27:30]:
            pltpu.make_async_remote_copy(
                src_ref=leaving.at[chunk, other],
                dst_ref=result.at[me, chunk],
                send_sem=out_send,
                recv_sem=out_recv,
                device_id={"wide": other},
                device_id_type=pl.DeviceIdType.MESH,
            ).start()
        pltpu.make_async_copy(leaving.at[chunk, me], result.at[me, chunk], own_sem.at[CHUNKS + chunk]).start()
        return carry

    lax.fori_loop(0, CHUNKS, one_chunk, 0)

    sent = given.at[pl.ds(0, WIDE - 1)]
    pltpu.make_async_copy(sent, sent, in_send).wait()
    for chunk in range(CHUNKS):
        pltpu.make_async_copy(leaving.at[chunk, me], result.at[me, chunk], own_sem.at[CHUNKS + chunk]).wait()
    arrived = result.at[pl.ds(0, WIDE - 1)]
    pltpu.make_async_copy(arrived, arrived, out_recv).wait()
    pltpu.make_async_copy(arrived, arrived, out_send).wait()


def run(given, gate_re, gate_im, bit_orders, phase_pairs, phase_angles):
    operands = (given, gate_re, gate_im, bit_orders, phase_pairs, phase_angles)
    return pl.pallas_call(
        kernel,
        out_shape=pltpu.VMEM(given.shape, jnp.float32),
        in_specs=[pl.BlockSpec(memory_space=pltpu.HBM)] * len(operands),
        out_specs=pl.BlockSpec(memory_space=pltpu.VMEM),
        scratch_shapes=[
            pltpu.VMEM(gate_re.shape, jnp.float32),
            pltpu.VMEM(gate_im.shape, jnp.float32),
            pltpu.SMEM(bit_orders.shape, jnp.int32),
            pltpu.SMEM(phase_pairs.shape, jnp.int32),
            pltpu.SMEM(phase_angles.shape, jnp.float32),
            pltpu.VMEM((CHUNKS, WIDE, 32, 128), jnp.float32),
            pltpu.VMEM((CHUNKS, WIDE, 32, 128), jnp.float32),
            pltpu.VMEM((4, 256, 128), jnp.float32),
            pltpu.VMEM((256, 512), jnp.float32),
            pltpu.VMEM((LAYERS, 512, 512), jnp.bfloat16),
            pltpu.VMEM((LAYERS, 512, 512), jnp.bfloat16),
            pltpu.VMEM((LAYERS, CHUNKS, 2, 8, 128), jnp.float32),
            pltpu.VMEM((LAYERS, CHUNKS, 2, 8, 128), jnp.float32),
            pltpu.SemaphoreType.DMA,
            pltpu.SemaphoreType.DMA((CHUNKS,)),
            pltpu.SemaphoreType.DMA,
            pltpu.SemaphoreType.DMA,
            pltpu.SemaphoreType.DMA((2 * CHUNKS,)),
            pltpu.SemaphoreType.DMA((5,)),
            pltpu.SemaphoreType.REGULAR((3,)),
        ],
        compiler_params=pltpu.CompilerParams(
            collective_id=0, has_side_effects=True, vmem_limit_bytes=48 * 1024 * 1024
        ),
        cost_estimate=pl.CostEstimate(flops=4_831_838_208, bytes_accessed=4_194_304, transcendentals=49_152),
    )(*[pltpu.with_memory_space_constraint(x, pltpu.HBM) for x in operands])


def local(state, gate_re, gate_im, bit_orders, phase_pairs, phase_angles):
    given = state.reshape(2, 1024, 128).transpose(1, 0, 2).reshape(WIDE, CHUNKS, 32, 128)
    result = run(given, gate_re, gate_im, bit_orders, phase_pairs.transpose(0, 2, 1), phase_angles)
    return result.reshape(1024, 2, 128).transpose(1, 0, 2).reshape(state.shape)


def solution(mesh):
    return jax.shard_map(
        local,
        mesh=mesh,
        in_specs=(P(None, ("wide", "narrow")), P(), P(), P(), P(), P()),
        out_specs=P(None, ("wide", "narrow")),
        check_vma=False,
    )
```
